32 devices in a mesh: section: 4 (over x, core), dp: 8 (over z, y).
Axes of the slice: x: 2, y: 2, z: 4, core: 2. Of those that a mesh axis runs over, the one named last changes fastest.
Arguments:
- embedded: bfloat16 [4, 256, 5120], P(None, 'dp'), may hold values from -6 to 6
- order: int32 [4], replicated, may hold values from 0 to 3, each once
- counts: int32 [4], P('section'), may hold values from 2 to 4, as said below
- gains: float32 [4, 4, 5120], P('section'), may hold values from 0.1 to 1.9
- mixers: bfloat16 [4, 4, 40, 128, 128], P('section'), may hold values from -0.5 to 0.5
- hidden_grads: bfloat16 [4, 4, 256, 13824], P('section', None, 'dp'), may hold values from -6 to 6
Outputs:
- input_factor: float32 [4, 64, 5120], P('section', 'dp')
- hidden_factor: float32 [4, 64, 13824], P('section', 'dp')
The draws below stay inside these ranges and needn't reach their ends.
Inputs may be any that keep to these rules, and one draw needn't show every extreme that they name: order is a permutation of the roster positions. `counts`: some section has exactly 4 layers.
All inputs are finite; a program needn't handle non-finite values.
Results may differ from the reference program's by a relative error of at most 0.0069.
Values may be sent and summed in bfloat16 or wider, within the bound.
A program may use at most 128 MiB of HBM per device.

```python
import jax
import jax.numpy as jnp
import numpy as np
from jax import lax

HEADS = 40
HD = 128
FF = 13824
D = 5120
MICRO = 4
LMAX = 4
SECTIONS = 4
TOKENS_MB = 256
AROWS = 64
GROWS = 64


def draw_counts(key, part):
    key = jax.random.fold_in(key, 7)
    first_key, second_key = jax.random.split(key)
    base = jax.random.randint(first_key, (SECTIONS,), 2, LMAX + 1)
    chosen = jax.random.randint(second_key, (), 0, SECTIONS)
    return jnp.where(jnp.arange(SECTIONS) == chosen, LMAX, base).astype(jnp.int32)


def levels(key, shape, cuts, low, high):
    loudness = 1.0
    for axis_at, shards_of in cuts:
        draws = jax.random.uniform(jax.random.fold_in(jax.random.fold_in(key, 6), axis_at), (shards_of,), jnp.float32, low / len(cuts), high / len(cuts))
        loudness = loudness * jnp.repeat(jnp.exp(draws), shape[axis_at] // shards_of).reshape((-1,) + (1,) * (len(shape) - 1 - axis_at))
    return loudness


def noise(rng, extent, spread, most, shards=(), held_as=jnp.bfloat16):
    gain = levels(rng, extent, shards, -0.22, 0.18) if shards else 1.0
    array = jax.random.normal(rng, extent, jnp.float32) * spread * gain
    return jnp.minimum(jnp.maximum(array, -most), most).astype(held_as)


def setup_inputs(seed: int = 0) -> dict:
    keys = jax.random.split(jax.random.key(seed), 7)
    embedded = noise(keys[0], (MICRO, TOKENS_MB, D), 1.0, 6.0, ((1, 8),))
    order = jax.random.permutation(keys[1], MICRO).astype(jnp.int32)
    counts = draw_counts(jax.random.fold_in(keys[6], 71), 0)
    gains = jnp.clip(1.0 + 0.18 * jax.random.normal(keys[3], (SECTIONS, LMAX, D), jnp.float32), 0.1, 1.9)
    mixers = noise(keys[4], (SECTIONS, LMAX, HEADS, HD, HD), HD ** -0.5, 0.5, ((0, 4),))
    hidden_grads = noise(keys[5], (SECTIONS, MICRO, TOKENS_MB, FF), 1.0, 6.0, ((0, 4), (2, 8)))
    return dict(embedded=embedded, order=order, counts=counts, gains=gains, mixers=mixers, hidden_grads=hidden_grads)


def normalize(values):
    return values * lax.rsqrt(lax.optimization_barrier(jnp.mean(values * values, axis=-1, keepdims=True)) + 1e-05)

def run_layers(hidden_in, count, gains, mixers):
    current = hidden_in.astype(jnp.float32)
    tokens_here = current.shape[0]
    for layer_index in range(LMAX):
        scaled = (normalize(current) * gains[layer_index]).astype(jnp.bfloat16)
        mixed = jnp.einsum('thi,hij->thj', scaled.reshape(tokens_here, HEADS, HD).astype(jnp.float32), mixers[layer_index].astype(jnp.float32))
        current = jnp.where(layer_index < count, current + mixed.reshape(tokens_here, D), current)
    return current.astype(jnp.bfloat16)

def reference(embedded, order, counts, gains, mixers, hidden_grads):
    position_weight = jnp.asarray(0.95 ** (MICRO - 1 - np.arange(MICRO)), jnp.float32)
    onehot = (order[:, None] == jnp.arange(MICRO, dtype=jnp.int32)[None, :]).astype(jnp.float32)
    batch_weight = jnp.dot(position_weight, onehot)
    input_rows = [jnp.zeros((AROWS, D), jnp.float32) for section_index in range(SECTIONS)]
    hidden_rows = [jnp.zeros((GROWS, FF), jnp.float32) for section_index in range(SECTIONS)]
    for micro_index in range(MICRO):
        hidden_state = embedded[micro_index]
        for section_index in range(SECTIONS):
            hidden_state = run_layers(hidden_state, counts[section_index], gains[section_index], mixers[section_index])
            normed = normalize(hidden_state.astype(jnp.float32)).astype(jnp.bfloat16)
            gram = jnp.dot(normed[:, :AROWS].T, normed, preferred_element_type=jnp.float32)
            input_rows[section_index] = input_rows[section_index] + batch_weight[micro_index] * gram
            grads = hidden_grads[section_index, micro_index]
            hidden_gram = jnp.dot(grads[:, :GROWS].T, grads, preferred_element_type=jnp.float32)
            hidden_rows[section_index] = hidden_rows[section_index] + batch_weight[micro_index] * hidden_gram
    input_factor = jnp.stack(input_rows) / TOKENS_MB
    hidden_factor = jnp.stack(hidden_rows) / TOKENS_MB
    return (input_factor, hidden_factor)
```

```python
import functools

import jax
import jax.numpy as jnp
import numpy as np
from jax import lax
from jax.experimental import pallas as pl
from jax.experimental.pallas import tpu as pltpu
from jax.sharding import PartitionSpec as P

ROWS_DEV = 8
TILE = 256
HIDDEN_CHUNKS = 3
INPUT_CHUNKS = 2
MESH = pl.DeviceIdType.MESH
EPS = 1e-05


def kernel(
    sizes,
    emb_hbm, order_ref, counts_ref, gains_hbm, mixers_hbm, grads_hbm,
    out_in, out_hid,
    mixers, gains, gains_of, grads, arrived, produced, state, normed, acc, left_t,
    part_h, half_h, sum_h, got_h, part_i, half_i, sum_i, got_i,
    mixer_sem, gains_sem, grads_sem, emb_sem,
    relay_send, relay_recv,
    send1_h, recv1_h, send2_h, recv2_h, send1_i, recv1_i, send2_i, recv2_i,
):
    sections, data_size, micro_count, tokens, width, layers, heads, head_size, hidden = sizes
    peers = data_size // 2
    rows = ROWS_DEV * data_size
    inverse = 1.0 / (tokens * data_size)
    sec = lax.axis_index("section")
    dp = lax.axis_index("dp")
    mine, lane = lax.div(dp, 2), lax.rem(dp, 2)
    partner = mine * 2 + (1 - lane)

    def emb_copy(m):
        return pltpu.make_async_copy(emb_hbm.at[m], arrived.at[m], emb_sem.at[m])

    def mixer_copy(l):
        return pltpu.make_async_copy(mixers_hbm.at[0, l], mixers.at[l], mixer_sem.at[l])

    gains_copy = pltpu.make_async_copy(gains_hbm.at[0], gains, gains_sem)
    grads_copy = pltpu.make_async_copy(grads_hbm.at[0], grads, grads_sem)

    barrier = pltpu.get_barrier_semaphore()

    @pl.when(sec > 0)
    def _():
        pl.semaphore_signal(barrier, inc=1, device_id={"section": sec - 1}, device_id_type=MESH)

    @pl.when(sec < sections - 1)
    def _():
        pl.semaphore_signal(barrier, inc=1, device_id={"section": sec + 1}, device_id_type=MESH)

    pl.semaphore_signal(barrier, inc=1, device_id={"dp": partner}, device_id_type=MESH)
    for step in range(1, peers):
        other = lax.rem(mine + step, peers)
        pl.semaphore_signal(barrier, inc=1, device_id={"dp": other * 2 + lane}, device_id_type=MESH)

    @pl.when(sec == 0)
    def _():
        for m in range(micro_count):
            emb_copy(m).start()

    @pl.when(sec > 0)
    def _():
        grads_copy.start()

    gains_copy.start()
    for l in range(layers):
        mixer_copy(l).start()

    @pl.when(sec == 0)
    def _():
        grads_copy.start()

    position_weight = (0.95 ** (micro_count - 1 - np.arange(micro_count))).astype(np.float32)

    def batch_weight(m):
        total = jnp.float32(0.0)
        for k in range(micro_count):
            total = total + jnp.where(order_ref[k] == m, jnp.float32(position_weight[k]), jnp.float32(0.0))
        return total

    acc[...] = jnp.zeros_like(acc)
    links = (sec > 0).astype(jnp.int32) + (sec < sections - 1).astype(jnp.int32) + peers
    pl.semaphore_wait(barrier, links)

    def store_parts(part, k, offset, low, high):
        for j in range(data_size):
            at = slice(j * ROWS_DEV, (j + 1) * ROWS_DEV)
            block = jnp.concatenate([low[at], high[at]], axis=0).astype(jnp.bfloat16)
            part[k, j % 2, j // 2, :, pl.ds(offset, TILE)] = block

    def first_copy(part, half, send, recv, k):
        return pltpu.make_async_remote_copy(
            src_ref=part.at[k, 1 - lane], dst_ref=half.at[k],
            send_sem=send.at[k], recv_sem=recv.at[k],
            device_id={"dp": partner}, device_id_type=MESH,
        )

    def second_copy(total, got, send, recv, k, other):
        return pltpu.make_async_remote_copy(
            src_ref=total.at[k, other], dst_ref=got.at[k, mine],
            send_sem=send.at[k, other], recv_sem=recv.at[k, mine],
            device_id={"dp": other * 2 + lane}, device_id_type=MESH,
        )

    def second_arrival(total, got, send, recv, k, other):
        return pltpu.make_async_remote_copy(
            src_ref=total.at[k, other], dst_ref=got.at[k, other],
            send_sem=send.at[k, other], recv_sem=recv.at[k, other],
            device_id={"dp": other * 2 + lane}, device_id_type=MESH,
        )

    def pass_on(k, part, half, total, got, send1, recv1, send2, recv2):
        first_copy(part, half, send1, recv1, k).wait_recv()
        for step in range(1, peers + 1):
            other = lax.rem(mine + step, peers)
            both = part[k, lane, other].astype(jnp.float32) + half[k, other].astype(jnp.float32)
            total[k, other] = both.astype(jnp.bfloat16)
            if step < peers:
                second_copy(total, got, send2, recv2, k, other).start()

    def finish(k, out, part, half, total, got, send1, recv1, send2, recv2):
        chunk = part.shape[-1]
        middle = out.shape[-1] // 2
        summed = total[k, mine].astype(jnp.float32)
        for step in range(1, peers):
            other = lax.rem(mine + step, peers)
            second_arrival(total, got, send2, recv2, k, other).wait_recv()
            summed = summed + got[k, other].astype(jnp.float32)
        summed = summed * inverse
        out[0, :, pl.ds(k * chunk, chunk)] = summed[:ROWS_DEV]
        out[0, :, pl.ds(middle + k * chunk, chunk)] = summed[ROWS_DEV:]

    def drain(k, part, half, total, got, send1, recv1, send2, recv2):
        first_copy(part, half, send1, recv1, k).wait_send()
        for step in range(1, peers):
            other = lax.rem(mine + step, peers)
            second_copy(total, got, send2, recv2, k, other).wait_send()

    of_hidden = (part_h, half_h, sum_h, got_h, send1_h, recv1_h, send2_h, recv2_h)
    of_input = (part_i, half_i, sum_i, got_i, send1_i, recv1_i, send2_i, recv2_i)
    chunk_h, chunk_i = part_h.shape[-1], part_i.shape[-1]

    def hidden_left():
        grads_copy.wait()
        for m in range(micro_count):
            left = grads[m, :, :rows].astype(jnp.float32)
            left_t[m] = jnp.transpose(left).astype(jnp.bfloat16)

    def hidden_gram(k):
        weights = [batch_weight(m) for m in range(micro_count)]

        def tile(i, carry):
            offset = pl.multiple_of(i * TILE, TILE)
            start = pl.multiple_of(k * chunk_h + i * TILE, TILE)
            sums = []
            for at in (start, start + hidden // 2):
                total = None
                for m in range(micro_count):
                    term = jnp.dot(
                        left_t[m], grads[m, :, pl.ds(pl.multiple_of(at, TILE), TILE)],
                        preferred_element_type=jnp.float32,
                    ) * weights[m]
                    total = term if total is None else total + term
                sums.append(total)
            store_parts(part_h, k, offset, *sums)
            return carry

        lax.fori_loop(0, chunk_h // TILE, tile, 0)
        first_copy(part_h, half_h, send1_h, recv1_h, k).start()

    @pl.when(sec > 0)
    def _():
        hidden_left()

        def one(k, carry):
            hidden_gram(k)
            return carry

        lax.fori_loop(0, HIDDEN_CHUNKS, one, 0)

    gains_copy.wait()
    for l in range(layers):
        gains_of[l] = jnp.broadcast_to(gains[l:l + 1, :], (8, width))

    def relay_copy(m):
        return pltpu.make_async_remote_copy(
            src_ref=produced.at[m], dst_ref=arrived.at[m],
            send_sem=relay_send.at[m], recv_sem=relay_recv.at[m],
            device_id={"section": lax.rem(sec + 1, sections)}, device_id_type=MESH,
        )

    def scale_of(squares):
        return lax.rsqrt(jnp.sum(squares, axis=-1, keepdims=True) * (1.0 / width) + EPS)

    def columns(g):
        return slice(g * head_size, (g + 1) * head_size)

    def micro(m, carry):
        @pl.when(sec == 0)
        def _():
            emb_copy(m).wait()

        @pl.when(sec > 0)
        def _():
            relay_copy(m).wait_recv()

        squares = jnp.zeros((tokens, head_size), jnp.float32)
        for g in range(heads):
            value = arrived[m, :, columns(g)].astype(jnp.float32)
            state[:, columns(g)] = value
            squares = squares + value * value

        def layer(l, squares):
            @pl.when(m == 0)
            def _():
                mixer_copy(l).wait()

            active = jnp.where(l < counts_ref[0], jnp.float32(1.0), jnp.float32(0.0))
            scale = scale_of(squares) * active
            after = jnp.zeros((tokens, head_size), jnp.float32)
            for g in range(heads):
                value = state[:, columns(g)]
                scaled = ((value * scale) * gains_of[l, 0:1, columns(g)]).astype(jnp.bfloat16)
                value = value + jnp.dot(scaled, mixers[l, g], preferred_element_type=jnp.float32)
                state[:, columns(g)] = value
                after = after + value * value
            return after

        lax.fori_loop(0, layers, layer, squares)

        squares = jnp.zeros((tokens, head_size), jnp.float32)
        for g in range(heads):
            value = state[:, columns(g)].astype(jnp.bfloat16)
            produced[m, :, columns(g)] = value
            value = value.astype(jnp.float32)
            squares = squares + value * value

        @pl.when(sec < sections - 1)
        def _():
            relay_copy(m).start()

        scale = scale_of(squares)
        for g in range(heads):
            value = produced[m, :, columns(g)].astype(jnp.float32) * scale
            normed[:, columns(g)] = value.astype(jnp.bfloat16)
        left = jnp.transpose(normed[:, :rows].astype(jnp.float32)).astype(jnp.bfloat16)
        weight = batch_weight(m)
        for at in range(0, width, TILE):
            term = jnp.dot(left, normed[:, at:at + TILE], preferred_element_type=jnp.float32)
            acc[:, at:at + TILE] += term * weight

        @pl.when(jnp.logical_and(sec == 0, m < HIDDEN_CHUNKS))
        def _():
            @pl.when(m == 0)
            def _():
                hidden_left()

            hidden_gram(m)

        @pl.when(jnp.logical_and(sec * 2 >= sections, m < HIDDEN_CHUNKS))
        def _():
            pass_on(m, *of_hidden)

        return carry

    lax.fori_loop(0, micro_count, micro, 0)

    for k in range(INPUT_CHUNKS):
        for i in range(chunk_i // TILE):
            at = k * chunk_i + i * TILE
            middle = at + width // 2
            store_parts(part_i, k, i * TILE, acc[:, at:at + TILE], acc[:, middle:middle + TILE])
        first_copy(part_i, half_i, send1_i, recv1_i, k).start()

    @pl.when(sec * 2 < sections)
    def _():
        def one(k, carry):
            pass_on(k, *of_hidden)
            return carry

        lax.fori_loop(0, HIDDEN_CHUNKS, one, 0)

    for k in range(INPUT_CHUNKS):
        pass_on(k, *of_input)
    for k in range(HIDDEN_CHUNKS):
        finish(k, out_hid, *of_hidden)
    for k in range(INPUT_CHUNKS):
        finish(k, out_in, *of_input)

    for k in range(HIDDEN_CHUNKS):
        drain(k, *of_hidden)
    for k in range(INPUT_CHUNKS):
        drain(k, *of_input)

    @pl.when(sec < sections - 1)
    def _():
        for m in range(micro_count):
            relay_copy(m).wait_send()


def body(embedded, order, counts, gains, mixers, hidden_grads):
    micro_count, tokens, width = embedded.shape
    _, layers, heads, head_size, _ = mixers.shape
    hidden = hidden_grads.shape[-1]
    sections, data_size = lax.axis_size("section"), lax.axis_size("dp")
    sizes = (sections, data_size, micro_count, tokens, width, layers, heads, head_size, hidden)
    peers = data_size // 2
    rows = ROWS_DEV * data_size

    def buffers(columns, chunks):
        chunk = columns // 2 // chunks
        tile = (2 * ROWS_DEV, chunk)
        return [
            pltpu.VMEM((chunks, 2, peers) + tile, jnp.bfloat16),
            pltpu.VMEM((chunks, peers) + tile, jnp.bfloat16),
            pltpu.VMEM((chunks, peers) + tile, jnp.bfloat16),
            pltpu.VMEM((chunks, peers) + tile, jnp.bfloat16),
        ]

    def semaphores(chunks):
        return [
            pltpu.SemaphoreType.DMA((chunks,)),
            pltpu.SemaphoreType.DMA((chunks,)),
            pltpu.SemaphoreType.DMA((chunks, peers)),
            pltpu.SemaphoreType.DMA((chunks, peers)),
        ]

    anywhere = pl.BlockSpec(memory_space=pl.ANY)
    scalars = pl.BlockSpec(memory_space=pltpu.SMEM)
    vmem = pl.BlockSpec(memory_space=pltpu.VMEM)
    return pl.pallas_call(
        functools.partial(kernel, sizes),
        out_shape=(
            jax.ShapeDtypeStruct((1, ROWS_DEV, width), jnp.float32),
            jax.ShapeDtypeStruct((1, ROWS_DEV, hidden), jnp.float32),
        ),
        in_specs=[anywhere, scalars, scalars, anywhere, anywhere, anywhere],
        out_specs=(vmem, vmem),
        scratch_shapes=[
            pltpu.VMEM((layers, heads, head_size, head_size), jnp.bfloat16),
            pltpu.VMEM((layers, width), jnp.float32),
            pltpu.VMEM((layers, 8, width), jnp.float32),
            pltpu.VMEM((micro_count, tokens, hidden), jnp.bfloat16),
            pltpu.VMEM((micro_count, tokens, width), jnp.bfloat16),
            pltpu.VMEM((micro_count, tokens, width), jnp.bfloat16),
            pltpu.VMEM((tokens, width), jnp.float32),
            pltpu.VMEM((tokens, width), jnp.bfloat16),
            pltpu.VMEM((rows, width), jnp.float32),
            pltpu.VMEM((micro_count, rows, tokens), jnp.bfloat16),
        ]
        + buffers(hidden, HIDDEN_CHUNKS)
        + buffers(width, INPUT_CHUNKS)
        + [
            pltpu.SemaphoreType.DMA((layers,)),
            pltpu.SemaphoreType.DMA,
            pltpu.SemaphoreType.DMA,
            pltpu.SemaphoreType.DMA((micro_count,)),
            pltpu.SemaphoreType.DMA((micro_count,)),
            pltpu.SemaphoreType.DMA((micro_count,)),
        ]
        + semaphores(HIDDEN_CHUNKS)
        + semaphores(INPUT_CHUNKS),
        compiler_params=pltpu.CompilerParams(
            collective_id=0, has_side_effects=True, vmem_limit_bytes=56 * 1024 * 1024
        ),
    )(embedded, order, counts, gains, mixers, hidden_grads)


def solution(mesh):
    placed = (
        P(None, "dp", None),
        P(),
        P("section"),
        P("section", None, None),
        P("section", None, None, None, None),
        P("section", None, "dp", None),
    )
    return jax.shard_map(
        body,
        mesh=mesh,
        in_specs=placed,
        out_specs=(P("section", "dp", None), P("section", "dp", None)),
        check_vma=False,
    )
```

```python
import functools

import jax
import jax.numpy as jnp
import numpy as np
from jax import lax
from jax.experimental import pallas as pl
from jax.experimental.pallas import tpu as pltpu
from jax.sharding import PartitionSpec as P

ROWS_DEV = 8
TILE = 256
HIDDEN_CHUNKS = 3
INPUT_CHUNKS = 2
MESH = pl.DeviceIdType.MESH
EPS = 1e-05


def kernel(
    sizes,
    emb_hbm, order_ref, counts_ref, gains_hbm, mixers_hbm, grads_hbm,
    out_in, out_hid,
    mixers, gains, gains_of, grads, arrived, produced, state, squared, normed, acc, left_t,
    part_h, half_h, sum_h, got_h, part_i, half_i, sum_i, got_i,
    mixer_sem, gains_sem, grads_sem, emb_sem,
    relay_send, relay_recv,
    send1_h, recv1_h, send2_h, recv2_h, send1_i, recv1_i, send2_i, recv2_i,
):
    sections, data_size, micro_count, tokens, width, layers, heads, head_size, hidden = sizes
    peers = data_size // 2
    rows = ROWS_DEV * data_size
    inverse = 1.0 / (tokens * data_size)
    sec = lax.axis_index("section")
    dp = lax.axis_index("dp")
    mine, lane = lax.div(dp, 2), lax.rem(dp, 2)
    partner = mine * 2 + (1 - lane)

    def emb_copy(m):
        return pltpu.make_async_copy(emb_hbm.at[m], arrived.at[m], emb_sem.at[m])

    def mixer_copy(l):
        return pltpu.make_async_copy(mixers_hbm.at[0, l], mixers.at[l], mixer_sem.at[l])

    gains_copy = pltpu.make_async_copy(gains_hbm.at[0], gains, gains_sem)
    grads_copy = pltpu.make_async_copy(grads_hbm.at[0], grads, grads_sem)

    barrier = pltpu.get_barrier_semaphore()

    @pl.when(sec > 0)
    def _():
        pl.semaphore_signal(barrier, inc=1, device_id={"section": sec - 1}, device_id_type=MESH)

    @pl.when(sec < sections - 1)
    def _():
        pl.semaphore_signal(barrier, inc=1, device_id={"section": sec + 1}, device_id_type=MESH)

    pl.semaphore_signal(barrier, inc=1, device_id={"dp": partner}, device_id_type=MESH)
    for step in range(1, peers):
        other = lax.rem(mine + step, peers)
        pl.semaphore_signal(barrier, inc=1, device_id={"dp": other * 2 + lane}, device_id_type=MESH)

    @pl.when(sec == 0)
    def _():
        for m in range(micro_count):
            emb_copy(m).start()

    @pl.when(sec > 0)
    def _():
        grads_copy.start()

    gains_copy.start()
    for l in range(layers):
        mixer_copy(l).start()

    @pl.when(sec == 0)
    def _():
        grads_copy.start()

    position_weight = (0.95 ** (micro_count - 1 - np.arange(micro_count))).astype(np.float32)

    def batch_weight(m):
        total = jnp.float32(0.0)
        for k in range(micro_count):
            total = total + jnp.where(order_ref[k] == m, jnp.float32(position_weight[k]), jnp.float32(0.0))
        return total

    acc[...] = jnp.zeros_like(acc)
    links = (sec > 0).astype(jnp.int32) + (sec < sections - 1).astype(jnp.int32) + peers
    pl.semaphore_wait(barrier, links)

    def store_parts(part, k, offset, low, high):
        for j in range(data_size):
            at = slice(j * ROWS_DEV, (j + 1) * ROWS_DEV)
            block = jnp.concatenate([low[at], high[at]], axis=0).astype(jnp.bfloat16)
            part[k, j % 2, j // 2, :, pl.ds(offset, TILE)] = block

    def first_copy(part, half, send, recv, k):
        return pltpu.make_async_remote_copy(
            src_ref=part.at[k, 1 - lane], dst_ref=half.at[k],
            send_sem=send.at[k], recv_sem=recv.at[k],
            device_id={"dp": partner}, device_id_type=MESH,
        )

    def second_copy(total, got, send, recv, k, other):
        return pltpu.make_async_remote_copy(
            src_ref=total.at[k, other], dst_ref=got.at[k, mine],
            send_sem=send.at[k, other], recv_sem=recv.at[k, mine],
            device_id={"dp": other * 2 + lane}, device_id_type=MESH,
        )

    def second_arrival(total, got, send, recv, k, other):
        return pltpu.make_async_remote_copy(
            src_ref=total.at[k, other], dst_ref=got.at[k, other],
            send_sem=send.at[k, other], recv_sem=recv.at[k, other],
            device_id={"dp": other * 2 + lane}, device_id_type=MESH,
        )

    def pass_on(k, part, half, total, got, send1, recv1, send2, recv2):
        first_copy(part, half, send1, recv1, k).wait_recv()
        for step in range(1, peers + 1):
            other = lax.rem(mine + step, peers)
            both = part[k, lane, other].astype(jnp.float32) + half[k, other].astype(jnp.float32)
            total[k, other] = both.astype(jnp.bfloat16)
            if step < peers:
                second_copy(total, got, send2, recv2, k, other).start()

    def finish(k, out, part, half, total, got, send1, recv1, send2, recv2):
        chunk = part.shape[-1]
        middle = out.shape[-1] // 2
        summed = total[k, mine].astype(jnp.float32)
        for step in range(1, peers):
            other = lax.rem(mine + step, peers)
            second_arrival(total, got, send2, recv2, k, other).wait_recv()
            summed = summed + got[k, other].astype(jnp.float32)
        summed = summed * inverse
        out[0, :, pl.ds(k * chunk, chunk)] = summed[:ROWS_DEV]
        out[0, :, pl.ds(middle + k * chunk, chunk)] = summed[ROWS_DEV:]

    def drain(k, part, half, total, got, send1, recv1, send2, recv2):
        first_copy(part, half, send1, recv1, k).wait_send()
        for step in range(1, peers):
            other = lax.rem(mine + step, peers)
            second_copy(total, got, send2, recv2, k, other).wait_send()

    of_hidden = (part_h, half_h, sum_h, got_h, send1_h, recv1_h, send2_h, recv2_h)
    of_input = (part_i, half_i, sum_i, got_i, send1_i, recv1_i, send2_i, recv2_i)
    chunk_h, chunk_i = part_h.shape[-1], part_i.shape[-1]

    def hidden_left():
        grads_copy.wait()
        for m in range(micro_count):
            left = grads[m, :, :rows].astype(jnp.float32)
            left_t[m] = jnp.transpose(left).astype(jnp.bfloat16)

    def hidden_gram(k):
        weights = [batch_weight(m) for m in range(micro_count)]

        def tile(i, carry):
            offset = pl.multiple_of(i * TILE, TILE)
            start = pl.multiple_of(k * chunk_h + i * TILE, TILE)
            sums = []
            for at in (start, start + hidden // 2):
                total = None
                for m in range(micro_count):
                    term = jnp.dot(
                        left_t[m], grads[m, :, pl.ds(pl.multiple_of(at, TILE), TILE)],
                        preferred_element_type=jnp.float32,
                    ) * weights[m]
                    total = term if total is None else total + term
                sums.append(total)
            store_parts(part_h, k, offset, *sums)
            return carry

        lax.fori_loop(0, chunk_h // TILE, tile, 0)
        first_copy(part_h, half_h, send1_h, recv1_h, k).start()

    early = sec * 2 < sections
    before = jnp.where(sec == 0, 0, jnp.where(early, HIDDEN_CHUNKS - 1, HIDDEN_CHUNKS))
    passed = jnp.where(sec == 0, 0, jnp.where(early, 1, jnp.where(sec == sections - 1, HIDDEN_CHUNKS, HIDDEN_CHUNKS - 1)))

    def hidden_part(k, carry):
        hidden_gram(k)
        return carry

    def pass_hidden(k, carry):
        pass_on(k, *of_hidden)
        return carry

    @pl.when(sec > 0)
    def _():
        hidden_left()
        lax.fori_loop(0, before, hidden_part, 0)

    gains_copy.wait()
    for l in range(layers):
        gains_of[l] = jnp.broadcast_to(gains[l:l + 1, :], (8, width))

    def relay_copy(m):
        return pltpu.make_async_remote_copy(
            src_ref=produced.at[m], dst_ref=arrived.at[m],
            send_sem=relay_send.at[m], recv_sem=relay_recv.at[m],
            device_id={"section": lax.rem(sec + 1, sections)}, device_id_type=MESH,
        )

    def scale_of(squares):
        return lax.rsqrt(jnp.sum(squares, axis=-1, keepdims=True) * (1.0 / width) + EPS)

    def columns(g):
        return slice(g * head_size, (g + 1) * head_size)

    def micro(m, carry):
        @pl.when(sec == 0)
        def _():
            emb_copy(m).wait()

        @pl.when(sec > 0)
        def _():
            relay_copy(m).wait_recv()

        squares = jnp.zeros((tokens, head_size), jnp.float32)
        for g in range(heads):
            value = arrived[m, :, columns(g)].astype(jnp.float32)
            state[:, columns(g)] = value
            squares = squares + value * value

        def layer(l, squares):
            @pl.when(m == 0)
            def _():
                mixer_copy(l).wait()

            active = jnp.where(l < counts_ref[0], jnp.float32(1.0), jnp.float32(0.0))
            scale = scale_of(squares) * active
            after = jnp.zeros((tokens, head_size), jnp.float32)
            for g in range(heads):
                value = state[:, columns(g)]
                scaled = ((value * scale) * gains_of[l, 0:1, columns(g)]).astype(jnp.bfloat16)
                value = value + jnp.dot(scaled, mixers[l, g], preferred_element_type=jnp.float32)
                state[:, columns(g)] = value
                after = after + value * value
            return after

        lax.fori_loop(0, layers, layer, squares)

        squares = jnp.zeros((tokens, head_size), jnp.float32)
        for g in range(heads):
            value = state[:, columns(g)].astype(jnp.bfloat16)
            produced[m, :, columns(g)] = value
            value = value.astype(jnp.float32)
            squares = squares + value * value

        squared[m] = squares

        @pl.when(sec < sections - 1)
        def _():
            relay_copy(m).start()

        @pl.when(jnp.logical_not(early))
        def _():
            statistics(m)

        @pl.when(jnp.logical_and(jnp.logical_not(early), m < passed))
        def _():
            pass_on(m, *of_hidden)

        return carry

    def statistics(m):
        scale = scale_of(squared[m])
        for g in range(heads):
            value = produced[m, :, columns(g)].astype(jnp.float32) * scale
            normed[:, columns(g)] = value.astype(jnp.bfloat16)
        left = jnp.transpose(normed[:, :rows].astype(jnp.float32)).astype(jnp.bfloat16)
        weight = batch_weight(m)
        for at in range(0, width, TILE):
            term = jnp.dot(left, normed[:, at:at + TILE], preferred_element_type=jnp.float32)
            acc[:, at:at + TILE] += term * weight

    lax.fori_loop(0, micro_count, micro, 0)

    @pl.when(early)
    def _():
        @pl.when(sec == 0)
        def _():
            hidden_left()

        lax.fori_loop(before, HIDDEN_CHUNKS, hidden_part, 0)
        lax.fori_loop(0, passed, pass_hidden, 0)
        lax.fori_loop(0, micro_count, lambda m, carry: (statistics(m), carry)[1], 0)

    for k in range(INPUT_CHUNKS):
        for i in range(chunk_i // TILE):
            at = k * chunk_i + i * TILE
            middle = at + width // 2
            store_parts(part_i, k, i * TILE, acc[:, at:at + TILE], acc[:, middle:middle + TILE])
        first_copy(part_i, half_i, send1_i, recv1_i, k).start()

    lax.fori_loop(passed, HIDDEN_CHUNKS, pass_hidden, 0)
    for k in range(HIDDEN_CHUNKS - 1):
        finish(k, out_hid, *of_hidden)
    for k in range(INPUT_CHUNKS):
        pass_on(k, *of_input)
    finish(HIDDEN_CHUNKS - 1, out_hid, *of_hidden)
    for k in range(INPUT_CHUNKS):
        finish(k, out_in, *of_input)

    for k in range(HIDDEN_CHUNKS):
        drain(k, *of_hidden)
    for k in range(INPUT_CHUNKS):
        drain(k, *of_input)

    @pl.when(sec < sections - 1)
    def _():
        for m in range(micro_count):
            relay_copy(m).wait_send()


def body(embedded, order, counts, gains, mixers, hidden_grads):
    micro_count, tokens, width = embedded.shape
    _, layers, heads, head_size, _ = mixers.shape
    hidden = hidden_grads.shape[-1]
    sections, data_size = lax.axis_size("section"), lax.axis_size("dp")
    sizes = (sections, data_size, micro_count, tokens, width, layers, heads, head_size, hidden)
    peers = data_size // 2
    rows = ROWS_DEV * data_size

    def buffers(columns, chunks):
        chunk = columns // 2 // chunks
        tile = (2 * ROWS_DEV, chunk)
        return [
            pltpu.VMEM((chunks, 2, peers) + tile, jnp.bfloat16),
            pltpu.VMEM((chunks, peers) + tile, jnp.bfloat16),
            pltpu.VMEM((chunks, peers) + tile, jnp.bfloat16),
            pltpu.VMEM((chunks, peers) + tile, jnp.bfloat16),
        ]

    def semaphores(chunks):
        return [
            pltpu.SemaphoreType.DMA((chunks,)),
            pltpu.SemaphoreType.DMA((chunks,)),
            pltpu.SemaphoreType.DMA((chunks, peers)),
            pltpu.SemaphoreType.DMA((chunks, peers)),
        ]

    anywhere = pl.BlockSpec(memory_space=pl.ANY)
    scalars = pl.BlockSpec(memory_space=pltpu.SMEM)
    vmem = pl.BlockSpec(memory_space=pltpu.VMEM)
    return pl.pallas_call(
        functools.partial(kernel, sizes),
        out_shape=(
            jax.ShapeDtypeStruct((1, ROWS_DEV, width), jnp.float32),
            jax.ShapeDtypeStruct((1, ROWS_DEV, hidden), jnp.float32),
        ),
        in_specs=[anywhere, scalars, scalars, anywhere, anywhere, anywhere],
        out_specs=(vmem, vmem),
        scratch_shapes=[
            pltpu.VMEM((layers, heads, head_size, head_size), jnp.bfloat16),
            pltpu.VMEM((layers, width), jnp.float32),
            pltpu.VMEM((layers, 8, width), jnp.float32),
            pltpu.VMEM((micro_count, tokens, hidden), jnp.bfloat16),
            pltpu.VMEM((micro_count, tokens, width), jnp.bfloat16),
            pltpu.VMEM((micro_count, tokens, width), jnp.bfloat16),
            pltpu.VMEM((tokens, width), jnp.float32),
            pltpu.VMEM((micro_count, tokens, head_size), jnp.float32),
            pltpu.VMEM((tokens, width), jnp.bfloat16),
            pltpu.VMEM((rows, width), jnp.float32),
            pltpu.VMEM((micro_count, rows, tokens), jnp.bfloat16),
        ]
        + buffers(hidden, HIDDEN_CHUNKS)
        + buffers(width, INPUT_CHUNKS)
        + [
            pltpu.SemaphoreType.DMA((layers,)),
            pltpu.SemaphoreType.DMA,
            pltpu.SemaphoreType.DMA,
            pltpu.SemaphoreType.DMA((micro_count,)),
            pltpu.SemaphoreType.DMA((micro_count,)),
            pltpu.SemaphoreType.DMA((micro_count,)),
        ]
        + semaphores(HIDDEN_CHUNKS)
        + semaphores(INPUT_CHUNKS),
        compiler_params=pltpu.CompilerParams(
            collective_id=0, has_side_effects=True, vmem_limit_bytes=56 * 1024 * 1024
        ),
    )(embedded, order, counts, gains, mixers, hidden_grads)


def solution(mesh):
    placed = (
        P(None, "dp", None),
        P(),
        P("section"),
        P("section", None, None),
        P("section", None, None, None, None),
        P("section", None, "dp", None),
    )
    return jax.shard_map(
        body,
        mesh=mesh,
        in_specs=placed,
        out_specs=(P("section", "dp", None), P("section", "dp", None)),
        check_vma=False,
    )
```

```python
import functools

import jax
import jax.numpy as jnp
import numpy as np
from jax import lax
from jax.experimental import pallas as pl
from jax.experimental.pallas import tpu as pltpu
from jax.sharding import PartitionSpec as P

ROWS_DEV = 8
TILE = 256
HIDDEN_CHUNKS = 9
INPUT_CHUNKS = 2
MESH = pl.DeviceIdType.MESH
EPS = 1e-05


def kernel(
    sizes,
    emb_hbm, order_ref, counts_ref, gains_hbm, mixers_hbm, grads_hbm,
    out_in, out_hid,
    mixers, gains, gains_of, grads, arrived, produced, state, squared, normed, acc, left_t,
    part_h, half_h, sum_h, got_h, part_i, half_i, sum_i, got_i,
    mixer_sem, gains_sem, grads_sem, emb_sem,
    relay_send, relay_recv,
    send1_h, recv1_h, send2_h, recv2_h, send1_i, recv1_i, send2_i, recv2_i,
):
    sections, data_size, micro_count, tokens, width, layers, heads, head_size, hidden = sizes
    peers = data_size // 2
    rows = ROWS_DEV * data_size
    inverse = 1.0 / (tokens * data_size)
    sec = lax.axis_index("section")
    dp = lax.axis_index("dp")
    mine, lane = lax.div(dp, 2), lax.rem(dp, 2)
    partner = mine * 2 + (1 - lane)

    def emb_copy(m):
        return pltpu.make_async_copy(emb_hbm.at[m], arrived.at[m], emb_sem.at[m])

    def mixer_copy(l):
        return pltpu.make_async_copy(mixers_hbm.at[0, l], mixers.at[l], mixer_sem.at[l])

    gains_copy = pltpu.make_async_copy(gains_hbm.at[0], gains, gains_sem)
    grads_copy = pltpu.make_async_copy(grads_hbm.at[0], grads, grads_sem)

    barrier = pltpu.get_barrier_semaphore()

    @pl.when(sec > 0)
    def _():
        pl.semaphore_signal(barrier, inc=1, device_id={"section": sec - 1}, device_id_type=MESH)

    @pl.when(sec < sections - 1)
    def _():
        pl.semaphore_signal(barrier, inc=1, device_id={"section": sec + 1}, device_id_type=MESH)

    pl.semaphore_signal(barrier, inc=1, device_id={"dp": partner}, device_id_type=MESH)
    for step in range(1, peers):
        other = lax.rem(mine + step, peers)
        pl.semaphore_signal(barrier, inc=1, device_id={"dp": other * 2 + lane}, device_id_type=MESH)

    @pl.when(sec == 0)
    def _():
        for m in range(micro_count):
            emb_copy(m).start()

    @pl.when(sec > 0)
    def _():
        grads_copy.start()

    gains_copy.start()
    for l in range(layers):
        mixer_copy(l).start()

    @pl.when(sec == 0)
    def _():
        grads_copy.start()

    position_weight = (0.95 ** (micro_count - 1 - np.arange(micro_count))).astype(np.float32)

    def batch_weight(m):
        total = jnp.float32(0.0)
        for k in range(micro_count):
            total = total + jnp.where(order_ref[k] == m, jnp.float32(position_weight[k]), jnp.float32(0.0))
        return total

    acc[...] = jnp.zeros_like(acc)
    links = (sec > 0).astype(jnp.int32) + (sec < sections - 1).astype(jnp.int32) + peers
    pl.semaphore_wait(barrier, links)

    def store_parts(part, k, offset, low, high):
        for j in range(data_size):
            at = slice(j * ROWS_DEV, (j + 1) * ROWS_DEV)
            block = jnp.concatenate([low[at], high[at]], axis=0).astype(jnp.bfloat16)
            part[k, j % 2, j // 2, :, pl.ds(offset, TILE)] = block

    def first_copy(part, half, send, recv, k):
        return pltpu.make_async_remote_copy(
            src_ref=part.at[k, 1 - lane], dst_ref=half.at[k],
            send_sem=send.at[k], recv_sem=recv.at[k],
            device_id={"dp": partner}, device_id_type=MESH,
        )

    def second_copy(total, got, send, recv, k, other):
        return pltpu.make_async_remote_copy(
            src_ref=total.at[k, other], dst_ref=got.at[k, mine],
            send_sem=send.at[k, other], recv_sem=recv.at[k, mine],
            device_id={"dp": other * 2 + lane}, device_id_type=MESH,
        )

    def second_arrival(total, got, send, recv, k, other):
        return pltpu.make_async_remote_copy(
            src_ref=total.at[k, other], dst_ref=got.at[k, other],
            send_sem=send.at[k, other], recv_sem=recv.at[k, other],
            device_id={"dp": other * 2 + lane}, device_id_type=MESH,
        )

    def pass_on(k, part, half, total, got, send1, recv1, send2, recv2):
        first_copy(part, half, send1, recv1, k).wait_recv()
        for step in range(1, peers + 1):
            other = lax.rem(mine + step, peers)
            both = part[k, lane, other].astype(jnp.float32) + half[k, other].astype(jnp.float32)
            total[k, other] = both.astype(jnp.bfloat16)
            if step < peers:
                second_copy(total, got, send2, recv2, k, other).start()

    def finish(k, out, part, half, total, got, send1, recv1, send2, recv2):
        chunk = part.shape[-1]
        middle = out.shape[-1] // 2
        summed = total[k, mine].astype(jnp.float32)
        for step in range(1, peers):
            other = lax.rem(mine + step, peers)
            second_arrival(total, got, send2, recv2, k, other).wait_recv()
            summed = summed + got[k, other].astype(jnp.float32)
        summed = summed * inverse
        out[0, :, pl.ds(pl.multiple_of(k * chunk, TILE), chunk)] = summed[:ROWS_DEV]
        out[0, :, pl.ds(pl.multiple_of(middle + k * chunk, TILE), chunk)] = summed[ROWS_DEV:]

    def drain(k, part, half, total, got, send1, recv1, send2, recv2):
        first_copy(part, half, send1, recv1, k).wait_send()
        for step in range(1, peers):
            other = lax.rem(mine + step, peers)
            second_copy(total, got, send2, recv2, k, other).wait_send()

    of_hidden = (part_h, half_h, sum_h, got_h, send1_h, recv1_h, send2_h, recv2_h)
    of_input = (part_i, half_i, sum_i, got_i, send1_i, recv1_i, send2_i, recv2_i)
    chunk_h, chunk_i = part_h.shape[-1], part_i.shape[-1]

    def hidden_left():
        grads_copy.wait()
        for m in range(micro_count):
            left = grads[m, :, :rows].astype(jnp.float32)
            left_t[m] = jnp.transpose(left).astype(jnp.bfloat16)

    def hidden_gram(k):
        weights = [batch_weight(m) for m in range(micro_count)]

        def tile(i, carry):
            offset = pl.multiple_of(i * TILE, TILE)
            start = pl.multiple_of(k * chunk_h + i * TILE, TILE)
            sums = []
            for at in (start, start + hidden // 2):
                total = None
                for m in range(micro_count):
                    term = jnp.dot(
                        left_t[m], grads[m, :, pl.ds(pl.multiple_of(at, TILE), TILE)],
                        preferred_element_type=jnp.float32,
                    ) * weights[m]
                    total = term if total is None else total + term
                sums.append(total)
            store_parts(part_h, k, offset, *sums)
            return carry

        lax.fori_loop(0, chunk_h // TILE, tile, 0)
        first_copy(part_h, half_h, send1_h, recv1_h, k).start()

    early = sec * 2 < sections
    last = sec == sections - 1
    first = sec == 0

    def plan(at_first, at_early, at_late, at_last):
        late = jnp.where(last, at_last, at_late)
        return jnp.where(first, at_first, jnp.where(early, at_early, late))

    before = plan(0, 6, HIDDEN_CHUNKS, HIDDEN_CHUNKS)
    waiting, base, most = plan(0, 0, 2, 4), plan(0, 2, 3, 6), plan(0, 5, 7, HIDDEN_CHUNKS)
    passed = plan(3, 6, 7, HIDDEN_CHUNKS)

    def passed_by(m):
        return jnp.where(m == 0, waiting, jnp.minimum(base + 2 * (m - 1), most))

    def hidden_part(k, carry):
        hidden_gram(k)
        return carry

    def pass_hidden(k, carry):
        pass_on(k, *of_hidden)
        return carry

    @pl.when(sec > 0)
    def _():
        hidden_left()
        lax.fori_loop(0, before, hidden_part, 0)
        lax.fori_loop(0, waiting, pass_hidden, 0)

    gains_copy.wait()
    for l in range(layers):
        gains_of[l] = jnp.broadcast_to(gains[l:l + 1, :], (8, width))

    def relay_copy(m):
        return pltpu.make_async_remote_copy(
            src_ref=produced.at[m], dst_ref=arrived.at[m],
            send_sem=relay_send.at[m], recv_sem=relay_recv.at[m],
            device_id={"section": lax.rem(sec + 1, sections)}, device_id_type=MESH,
        )

    def scale_of(squares):
        return lax.rsqrt(jnp.sum(squares, axis=-1, keepdims=True) * (1.0 / width) + EPS)

    def columns(g):
        return slice(g * head_size, (g + 1) * head_size)

    def micro(m, carry):
        @pl.when(sec == 0)
        def _():
            emb_copy(m).wait()

        @pl.when(sec > 0)
        def _():
            relay_copy(m).wait_recv()

        squares = jnp.zeros((tokens, head_size), jnp.float32)
        for g in range(heads):
            value = arrived[m, :, columns(g)].astype(jnp.float32)
            state[:, columns(g)] = value
            squares = squares + value * value

        def layer(l, squares):
            @pl.when(m == 0)
            def _():
                mixer_copy(l).wait()

            active = jnp.where(l < counts_ref[0], jnp.float32(1.0), jnp.float32(0.0))
            scale = scale_of(squares) * active
            after = jnp.zeros((tokens, head_size), jnp.float32)
            for g in range(heads):
                value = state[:, columns(g)]
                scaled = ((value * scale) * gains_of[l, 0:1, columns(g)]).astype(jnp.bfloat16)
                value = value + jnp.dot(scaled, mixers[l, g], preferred_element_type=jnp.float32)
                state[:, columns(g)] = value
                after = after + value * value
            return after

        lax.fori_loop(0, layers, layer, squares)

        squares = jnp.zeros((tokens, head_size), jnp.float32)
        for g in range(heads):
            value = state[:, columns(g)].astype(jnp.bfloat16)
            produced[m, :, columns(g)] = value
            value = value.astype(jnp.float32)
            squares = squares + value * value

        squared[m] = squares

        @pl.when(sec < sections - 1)
        def _():
            relay_copy(m).start()

        @pl.when(jnp.logical_not(early))
        def _():
            statistics(m)

        @pl.when(jnp.logical_and(first, m > 0))
        def _():
            @pl.when(m == 1)
            def _():
                hidden_left()

            lax.fori_loop(HIDDEN_CHUNKS // 3 * (m - 1), HIDDEN_CHUNKS // 3 * m, hidden_part, 0)

        lax.fori_loop(passed_by(m), passed_by(m + 1), pass_hidden, 0)

        return carry

    def statistics(m):
        scale = scale_of(squared[m])
        for g in range(heads):
            value = produced[m, :, columns(g)].astype(jnp.float32) * scale
            normed[:, columns(g)] = value.astype(jnp.bfloat16)
        left = jnp.transpose(normed[:, :rows].astype(jnp.float32)).astype(jnp.bfloat16)
        weight = batch_weight(m)
        for at in range(0, width, TILE):
            term = jnp.dot(left, normed[:, at:at + TILE], preferred_element_type=jnp.float32)
            acc[:, at:at + TILE] += term * weight

    lax.fori_loop(0, micro_count, micro, 0)

    @pl.when(early)
    def _():
        lax.fori_loop(jnp.where(first, HIDDEN_CHUNKS, before), HIDDEN_CHUNKS, hidden_part, 0)
        lax.fori_loop(most, passed, pass_hidden, 0)
        lax.fori_loop(0, micro_count, lambda m, carry: (statistics(m), carry)[1], 0)

    for k in range(INPUT_CHUNKS):
        for i in range(chunk_i // TILE):
            at = k * chunk_i + i * TILE
            middle = at + width // 2
            store_parts(part_i, k, i * TILE, acc[:, at:at + TILE], acc[:, middle:middle + TILE])
        first_copy(part_i, half_i, send1_i, recv1_i, k).start()

    lax.fori_loop(passed, HIDDEN_CHUNKS, pass_hidden, 0)
    def finish_hidden(k, carry):
        finish(k, out_hid, *of_hidden)
        return carry

    def pass_input(k, carry):
        pass_on(k, *of_input)
        return carry

    def finish_input(k, carry):
        finish(k, out_in, *of_input)
        return carry

    def drain_hidden(k, carry):
        drain(k, *of_hidden)
        return carry

    def drain_input(k, carry):
        drain(k, *of_input)
        return carry

    lax.fori_loop(0, INPUT_CHUNKS, pass_input, 0)
    lax.fori_loop(0, HIDDEN_CHUNKS, finish_hidden, 0)
    lax.fori_loop(0, INPUT_CHUNKS, finish_input, 0)
    lax.fori_loop(0, HIDDEN_CHUNKS, drain_hidden, 0)
    lax.fori_loop(0, INPUT_CHUNKS, drain_input, 0)

    @pl.when(sec < sections - 1)
    def _():
        for m in range(micro_count):
            relay_copy(m).wait_send()


def body(embedded, order, counts, gains, mixers, hidden_grads):
    micro_count, tokens, width = embedded.shape
    _, layers, heads, head_size, _ = mixers.shape
    hidden = hidden_grads.shape[-1]
    sections, data_size = lax.axis_size("section"), lax.axis_size("dp")
    sizes = (sections, data_size, micro_count, tokens, width, layers, heads, head_size, hidden)
    peers = data_size // 2
    rows = ROWS_DEV * data_size

    def buffers(columns, chunks):
        chunk = columns // 2 // chunks
        tile = (2 * ROWS_DEV, chunk)
        return [
            pltpu.VMEM((chunks, 2, peers) + tile, jnp.bfloat16),
            pltpu.VMEM((chunks, peers) + tile, jnp.bfloat16),
            pltpu.VMEM((chunks, peers) + tile, jnp.bfloat16),
            pltpu.VMEM((chunks, peers) + tile, jnp.bfloat16),
        ]

    def semaphores(chunks):
        return [
            pltpu.SemaphoreType.DMA((chunks,)),
            pltpu.SemaphoreType.DMA((chunks,)),
            pltpu.SemaphoreType.DMA((chunks, peers)),
            pltpu.SemaphoreType.DMA((chunks, peers)),
        ]

    anywhere = pl.BlockSpec(memory_space=pl.ANY)
    scalars = pl.BlockSpec(memory_space=pltpu.SMEM)
    vmem = pl.BlockSpec(memory_space=pltpu.VMEM)
    return pl.pallas_call(
        functools.partial(kernel, sizes),
        out_shape=(
            jax.ShapeDtypeStruct((1, ROWS_DEV, width), jnp.float32),
            jax.ShapeDtypeStruct((1, ROWS_DEV, hidden), jnp.float32),
        ),
        in_specs=[anywhere, scalars, scalars, anywhere, anywhere, anywhere],
        out_specs=(vmem, vmem),
        scratch_shapes=[
            pltpu.VMEM((layers, heads, head_size, head_size), jnp.bfloat16),
            pltpu.VMEM((layers, width), jnp.float32),
            pltpu.VMEM((layers, 8, width), jnp.float32),
            pltpu.VMEM((micro_count, tokens, hidden), jnp.bfloat16),
            pltpu.VMEM((micro_count, tokens, width), jnp.bfloat16),
            pltpu.VMEM((micro_count, tokens, width), jnp.bfloat16),
            pltpu.VMEM((tokens, width), jnp.float32),
            pltpu.VMEM((micro_count, tokens, head_size), jnp.float32),
            pltpu.VMEM((tokens, width), jnp.bfloat16),
            pltpu.VMEM((rows, width), jnp.float32),
            pltpu.VMEM((micro_count, rows, tokens), jnp.bfloat16),
        ]
        + buffers(hidden, HIDDEN_CHUNKS)
        + buffers(width, INPUT_CHUNKS)
        + [
            pltpu.SemaphoreType.DMA((layers,)),
            pltpu.SemaphoreType.DMA,
            pltpu.SemaphoreType.DMA,
            pltpu.SemaphoreType.DMA((micro_count,)),
            pltpu.SemaphoreType.DMA((micro_count,)),
            pltpu.SemaphoreType.DMA((micro_count,)),
        ]
        + semaphores(HIDDEN_CHUNKS)
        + semaphores(INPUT_CHUNKS),
        compiler_params=pltpu.CompilerParams(
            collective_id=0, has_side_effects=True, vmem_limit_bytes=56 * 1024 * 1024
        ),
    )(embedded, order, counts, gains, mixers, hidden_grads)


def solution(mesh):
    placed = (
        P(None, "dp", None),
        P(),
        P("section"),
        P("section", None, None),
        P("section", None, None, None, None),
        P("section", None, "dp", None),
    )
    return jax.shard_map(
        body,
        mesh=mesh,
        in_specs=placed,
        out_specs=(P("section", "dp", None), P("section", "dp", None)),
        check_vma=False,
    )
```
